128 devices in a mesh: dp: 16 (over y, z), section: 2 (over x_lo), tensor: 4 (over x_hi, core).
Axes of the slice: x: 4 (x_hi: 2, x_lo: 2; x = x_hi * 2 + x_lo), y: 4, z: 4, core: 2. Of those that a mesh axis runs over, the one named last changes fastest.
Arguments:
- tokens: int32 [32, 1024], P('dp'), may hold values from 0 to 255
- doc_lengths: int32 [32, 8], P('dp'), may hold values from 1 to 776, 1024 in all within a row
- byte_embed: bfloat16 [2, 256, 768], P('section'), may hold values from -6 to 6
- patch_maps: bfloat16 [2, 6144, 768], P('section'), may hold values from -0.125 to 0.125
- attn_gain: float32 [2, 768], P('section'), may hold values from 0.5 to 1.5
- attn_shift: float32 [2, 768], P('section'), may hold values from -3 to 3
- qkv_weight: bfloat16 [2, 768, 3, 768], P('section', None, None, 'tensor'), may hold values from -0.21875 to 0.21875
- out_weight: bfloat16 [2, 768, 768], P('section', 'tensor'), may hold values from -0.4375 to 0.4375
- mlp_gain: float32 [2, 768], P('section'), may hold values from 0.5 to 1.5
- mlp_shift: float32 [2, 768], P('section'), may hold values from -3 to 3
- up_weight: bfloat16 [2, 768, 3072], P('section', None, 'tensor'), may hold values from -0.21875 to 0.21875
- up_bias: float32 [2, 3072], P('section', 'tensor'), may hold values from -3 to 3
- down_weight: bfloat16 [2, 3072, 768], P('section', 'tensor'), may hold values from -0.15625 to 0.15625
- down_bias: float32 [2, 768], P('section'), may hold values from -3 to 3
- cotangent: float32 [32, 1024, 768], P('dp', 'tensor'), may hold values from -6 to 6
Outputs:
- global_out: bfloat16 [32, 128, 768], P('dp', 'tensor')
- local_out: bfloat16 [32, 1024, 768], P('dp', 'tensor', 'section')
- grad_byte_embed: float32 [2, 256, 768], P('section')
- grad_patch_maps: float32 [2, 6144, 768], P('section')
- grad_attn_gain: float32 [2, 768], P('section')
- grad_attn_shift: float32 [2, 768], P('section')
- grad_qkv_weight: float32 [2, 768, 3, 768], P('section', None, None, 'tensor')
- grad_out_weight: float32 [2, 768, 768], P('section', 'tensor')
- grad_mlp_gain: float32 [2, 768], P('section')
- grad_mlp_shift: float32 [2, 768], P('section')
- grad_up_weight: float32 [2, 768, 3072], P('section', None, 'tensor')
- grad_up_bias: float32 [2, 3072], P('section', 'tensor')
- grad_down_weight: float32 [2, 3072, 768], P('section', 'tensor')
- grad_down_bias: float32 [2, 768], P('section')
The draws below stay inside these ranges and needn't reach their ends.
Inputs may be any that keep to these rules, and one draw needn't show every extreme that they name: `doc_lengths`: in each pack the 8 lengths, in order, cover its 1024 bytes exactly; one of them is 776.
All inputs are finite; a program needn't handle non-finite values.
Results may differ from the reference program's by a relative error of at most 0.03.
Values may be sent and summed in bfloat16 or wider, within the bound.
No kernel may reach another device: no remote copies, remote signals or barrier semaphores. Data moves between devices by JAX's collectives and lax.ppermute only.
A program may use at most 320 MiB of HBM per device.

```python
import math
import jax
import jax.numpy as jnp
import numpy as np
from jax import lax

D = 768
HEADS = 12
HEAD_DIM = 64
FF = 3072
VOCAB = 256
PATCH = 8
PATCHES = 128
DOCS = 8
BYTES = 1024
LONGEST = 776
PACKS = 32


def touch_ends(values, key, low, high):
    shape = values.shape
    place = [jax.random.randint(jax.random.fold_in(key, axis), (), 0, shape[axis]) for axis in range(len(shape))]
    values = values.at[tuple(place)].set(low)
    longest = shape.index(max(shape))
    place[longest] = (place[longest] + 1) % shape[longest]
    return values.at[tuple(place)].set(high)


def shard_levels(stream_key, shape, cuts, smallest, high):
    def one(position, parts):
        heights = jax.random.uniform(jax.random.fold_in(jax.random.fold_in(stream_key, 6), position), (parts,), jnp.float32, smallest / len(cuts), high / len(cuts))
        return jnp.repeat(jnp.exp(heights), shape[position] // parts).reshape((-1,) + (1,) * (len(shape) - position - 1))

    loudness = one(*cuts[0])
    for cut in cuts[1:]:
        loudness = loudness * one(*cut)
    return loudness


def rank_bounds(count, slope):
    weights = [(1 << 20) // math.isqrt(rank ** slope) + 1 for rank in range(1, count + 1)]
    scale = 1 + sum(weights) // (1 << 30)
    return np.cumsum(np.array([max(1, weight // scale) for weight in weights]))


def ranked(rng, shape, number_of, slope):
    grid = rank_bounds(number_of, slope)
    ticket = jax.random.randint(jax.random.fold_in(rng, 1), shape, 0, int(grid[number_of - 1]))
    grade = jnp.searchsorted(jnp.asarray(grid, jnp.int32), ticket, side="right")
    return jax.random.permutation(jax.random.fold_in(rng, 2), number_of)[grade].astype(jnp.int32)


def split_up(count, total, limit, lean):
    loads = [(1 << 20) // math.isqrt(grade ** lean) + 1 for grade in range(2, count + 1)]
    rest, given = total - limit - (count - 1), [1] * (count - 1)
    while rest > 0:
        candidates = [i for i in range(count - 1) if given[i] < limit]
        pool, budget = sum([loads[i] for i in candidates]), rest
        for i in candidates:
            extra = min(limit - given[i], max(1, budget * loads[i] // pool), rest)
            given[i] = given[i] + extra
            rest = rest - extra
    return np.array([limit] + given)


def uneven_parts(stream_key, number_of, total, reach, slope):
    if number_of == 2:
        one = jax.random.randint(stream_key, (), max(1, total - reach), min(reach, total - 1) + 1)
        return jnp.stack([one, total - one])
    sizes = jnp.asarray(split_up(number_of, total, reach, slope), jnp.int32)
    couples = (number_of - 1) // 2
    source_of, sink = sizes[1:1 + 2 * couples:2], sizes[2:2 + 2 * couples:2]
    room = jnp.minimum(source_of - 1, reach - sink)
    passed = jax.random.randint(jax.random.fold_in(stream_key, 1), (couples,), 0, 1 << 20) % (room + 1)
    sizes = sizes.at[1:1 + 2 * couples:2].set(source_of - passed).at[2:2 + 2 * couples:2].set(sink + passed)
    return sizes[jax.random.permutation(jax.random.fold_in(stream_key, 2), number_of)]


def gaussian(stream_key, shape, scale, reach, split=(), kind=jnp.bfloat16):
    level = shard_levels(stream_key, shape, split, -0.22, 0.18) if split else 1.0
    drawn = jax.random.normal(stream_key, shape, jnp.float32) * scale * level
    return jnp.minimum(jnp.maximum(drawn, -reach), reach).astype(kind)


def setup_inputs(seed: int = 0) -> dict:
    keys = jax.random.split(jax.random.key(seed), 16)
    return {
        "tokens": touch_ends(ranked(keys[0], (PACKS, BYTES), VOCAB, 2), jax.random.fold_in(keys[0], 3), 0, VOCAB - 1).astype(jnp.int32),
        "doc_lengths": jax.vmap(lambda own: uneven_parts(own, DOCS, BYTES, LONGEST, 2))(jax.random.split(keys[1], PACKS)).reshape((PACKS, DOCS)).astype(jnp.int32),
        "byte_embed": gaussian(keys[2], (2, VOCAB, D), 1.0, 6.0, ((0, 2),)),
        "patch_maps": gaussian(keys[3], (2, PATCH * D, D), (3 * D) ** -0.5, 0.125, ((0, 2),)),
        "attn_gain": jnp.clip(1.0 + 0.1 * jax.random.normal(keys[4], (2, D), jnp.float32), 0.5, 1.5),
        "attn_shift": gaussian(keys[5], (2, D), 0.5, 3.0, ((0, 2),), jnp.float32),
        "qkv_weight": gaussian(keys[6], (2, D, 3, D), D ** -0.5, 0.21875, ((0, 2), (3, 4))),
        "out_weight": gaussian(keys[7], (2, D, D), (D // 4) ** -0.5, 0.4375, ((0, 2), (1, 4))),
        "mlp_gain": jnp.clip(1.0 + 0.1 * jax.random.normal(keys[8], (2, D), jnp.float32), 0.5, 1.5),
        "mlp_shift": gaussian(keys[9], (2, D), 0.5, 3.0, ((0, 2),), jnp.float32),
        "up_weight": gaussian(keys[10], (2, D, FF), D ** -0.5, 0.21875, ((0, 2), (2, 4))),
        "up_bias": gaussian(keys[11], (2, FF), 0.5, 3.0, ((0, 2), (1, 4)), jnp.float32),
        "down_weight": gaussian(keys[12], (2, FF, D), (FF // 2) ** -0.5, 0.15625, ((0, 2), (1, 4))),
        "down_bias": gaussian(keys[13], (2, D), 0.5, 3.0, ((0, 2),), jnp.float32),
        "cotangent": gaussian(keys[14], (PACKS, BYTES, D), 1.0, 6.0, ((0, 16), (1, 4)), jnp.float32),
    }


@jax.custom_vjp
def low(v):
    return lax.optimization_barrier(v.astype(jnp.bfloat16)).astype(jnp.float32)

@jax.custom_vjp
def low_back(v):
    return v

def low_keep(v):
    return (low(v), None)

def low_pass(kept, grad):
    return (grad,)

def back_keep(v):
    return (v, None)

def back_low(kept, grad):
    return (low(grad),)
low.defvjp(low_keep, low_pass)
low_back.defvjp(back_keep, back_low)
EPSILON = 1e-05
PRECISE = lax.Precision.HIGHEST

def layer_norm(values, gain, shift):
    centered = values - lax.optimization_barrier(jnp.mean(values, axis=-1, keepdims=True))
    spread = lax.optimization_barrier(jnp.mean(centered * centered, axis=-1, keepdims=True))
    return centered * lax.rsqrt(spread + EPSILON) * gain + shift

def document_of(lengths, places):
    run_ends = jnp.cumsum(lengths)
    return lax.optimization_barrier(jnp.sum((run_ends[None, :] <= places[:, None]).astype(jnp.int32), axis=1))

def attention(queries, key_rows, value_rows, allowed):
    scores = jnp.einsum('gqhe,gkhe->ghqk', queries, key_rows, precision=PRECISE) * HEAD_DIM ** (-0.5)
    scores = low_back(scores)
    scores = jnp.where(allowed[:, None], scores, -jnp.inf)
    weights = low(jax.nn.softmax(scores, axis=-1))
    return jnp.einsum('ghqk,gkhe->gqhe', weights, value_rows, precision=PRECISE)

def block(stream_in, weights, allowed, grouped):
    attn_gain, attn_shift, qkv_weight, out_weight, mlp_gain, mlp_shift, up_weight, up_bias, down_weight, down_bias = weights
    row_count = stream_in.shape[0]
    normed = low(layer_norm(stream_in, attn_gain, attn_shift))
    mixed = jnp.dot(normed, qkv_weight.reshape(D, 3 * D), precision=PRECISE).reshape(row_count, 3, HEADS, HEAD_DIM)
    queries = low(low_back(mixed[:, 0])).reshape(grouped + (HEADS, HEAD_DIM))
    key_rows = low(low_back(mixed[:, 1])).reshape(grouped + (HEADS, HEAD_DIM))
    value_rows = low(low_back(mixed[:, 2])).reshape(grouped + (HEADS, HEAD_DIM))
    mixture = attention(queries, key_rows, value_rows, allowed).reshape(row_count, D)
    mixture = low(low_back(mixture))
    middle = stream_in + low_back(jnp.dot(mixture, out_weight, precision=PRECISE))
    normed_mlp = low(layer_norm(middle, mlp_gain, mlp_shift))
    upper = low_back(jnp.dot(normed_mlp, up_weight, precision=PRECISE) + up_bias)
    active = low(jax.nn.gelu(upper))
    return middle + low_back(jnp.dot(active, down_weight, precision=PRECISE) + down_bias)

def pack_forward(params, pack_tokens, pack_lengths):
    byte_embed = params[0]
    patch_maps = params[1]
    layer_weights = params[2:]
    places = jnp.arange(BYTES, dtype=jnp.int32)
    byte_docs = document_of(pack_lengths, places)
    patch_docs = byte_docs[::PATCH]
    patch_rank = jnp.arange(PATCHES, dtype=jnp.int32)
    global_allowed = ((patch_rank[None, :] <= patch_rank[:, None]) & (patch_docs[None, :] == patch_docs[:, None]))[None]
    in_patch = jnp.arange(PATCH, dtype=jnp.int32)
    grouped_docs = byte_docs.reshape(PATCHES, PATCH)
    local_allowed = (in_patch[None, :] <= in_patch[:, None])[None] & (grouped_docs[:, None, :] == grouped_docs[:, :, None])
    embedded = jnp.take(byte_embed[0], pack_tokens, axis=0).reshape(PATCHES, PATCH * D)
    patch_rows = jnp.concatenate([jnp.zeros((1, PATCH * D), jnp.float32), embedded[:-1]], axis=0)
    global_in = low_back(jnp.dot(patch_rows, patch_maps[0], precision=PRECISE))
    hidden = block(global_in, tuple((weight[0] for weight in layer_weights)), global_allowed, (1, PATCHES))
    hidden_low = low(low_back(hidden))
    stream = low_back(jnp.dot(hidden_low, patch_maps[1].T, precision=PRECISE).reshape(BYTES, D))
    grouped_tokens = pack_tokens.reshape(PATCHES, PATCH)
    earlier = jnp.concatenate([grouped_tokens[:, :1], grouped_tokens[:, :-1]], axis=1).reshape(BYTES)
    present = (places % PATCH != 0).astype(jnp.float32)
    local_in = jnp.take(byte_embed[1], earlier, axis=0) * present[:, None] + stream
    result = block(local_in, tuple((weight[1] for weight in layer_weights)), local_allowed, (PATCHES, PATCH))
    return (hidden_low, result)

def reference(tokens, doc_lengths, byte_embed, patch_maps, attn_gain, attn_shift, qkv_weight, out_weight, mlp_gain, mlp_shift, up_weight, up_bias, down_weight, down_bias, cotangent):
    params = tuple((weight.astype(jnp.float32) for weight in (byte_embed, patch_maps, attn_gain, attn_shift, qkv_weight, out_weight, mlp_gain, mlp_shift, up_weight, up_bias, down_weight, down_bias)))

    def one_pack(totals, pack_data):
        pack_tokens, pack_lengths, pack_grad = pack_data
        outputs, pull_back = jax.vjp(lambda chosen: pack_forward(chosen, pack_tokens, pack_lengths), params)
        grads, = pull_back((jnp.zeros_like(outputs[0]), pack_grad))
        return (tuple((a + b for a, b in zip(totals, grads))), outputs)
    starting = tuple((jnp.zeros_like(weight) for weight in params))
    totals, (hiddens, results) = lax.scan(one_pack, starting, (tokens, doc_lengths, cotangent))
    grad_embed, grad_maps, grad_attn_gain, grad_attn_shift, grad_qkv, grad_out, grad_mlp_gain, grad_mlp_shift, grad_up, grad_up_bias, grad_down, grad_down_bias = totals
    return (hiddens.astype(jnp.bfloat16), results.astype(jnp.bfloat16), grad_embed, grad_maps, grad_attn_gain, grad_attn_shift, grad_qkv, grad_out, grad_mlp_gain, grad_mlp_shift, grad_up, grad_up_bias, grad_down, grad_down_bias)
```

```python
from functools import partial

import jax
import jax.numpy as jnp
from jax import lax
from jax.sharding import PartitionSpec as P

HEAD_DIM = 64
PATCH = 8
WIDTH = 768
VOCAB = 256
EPSILON = 1e-05
SIDE = 4
TILE = 128
RELATIVE = (0, 2, 1, 3)
BF = jnp.bfloat16
F32 = jnp.float32


def send(value, move, sections=(0, 1)):
    def flat(y, z, s, t):
        return ((y % SIDE * SIDE + z % SIDE) * 2 + s) * 4 + t

    pairs = [
        (flat(y, z, s, t), flat(*move(y, z, s, t)))
        for y in range(SIDE)
        for z in range(SIDE)
        for s in sections
        for t in range(4)
    ]
    return lax.ppermute(value, ("dp", "section", "tensor"), pairs)


def to_core(value, section):
    return send(value, lambda y, z, s, t: (y, z, s, t ^ 1), (section,))


def to_chip(value, section):
    return send(value, lambda y, z, s, t: (y, z, s, t ^ 2), (section,))


def along(value, phase, step, section):
    def move(y, z, s, t):
        return (y + step, z, s, t) if t % 2 == phase else (y, z + step, s, t)

    return send(value, move, (section,))


def ring_place(phase):
    place = lax.axis_index("dp")
    core = lax.axis_index("tensor") % 2
    return jnp.where(core == phase, place // SIDE, place % SIDE)


def added(*parts):
    total = parts[0].astype(F32)
    for part in parts[1:]:
        total = total + part.astype(F32)
    return total.astype(BF)


def half_of(count):
    return (count // 2 + 7) // 8 * 8


def unwritten(*shapes):
    return [jnp.zeros(shape.shape, shape.dtype) for shape in shapes]


def ring_reduce(blocks, phase, section):
    place = ring_place(phase)
    half = half_of(blocks.shape[2])

    def block(steps):
        return lax.dynamic_index_in_dim(blocks, (place + steps) % SIDE, 1, keepdims=False)

    far, right, left = block(2), block(1), block(3)
    upper = along(far[:, :half], phase, 1, section)
    lower = along(far[:, half:], phase, -1, section)
    right = jnp.concatenate([added(right[:, :half], upper), right[:, half:]], axis=1)
    left = jnp.concatenate([left[:, :half], added(left[:, half:], lower)], axis=1)
    from_left = along(right, phase, 1, section)
    from_right = along(left, phase, -1, section)
    return added(block(0), from_left, from_right)


def ring_pieces(piece, phase, section, half=None):
    half = half or half_of(piece.shape[0])
    from_left = along(piece, phase, 1, section)
    from_right = along(piece, phase, -1, section)
    upper = along(from_left[:half], phase, 1, section)
    lower = along(from_right[half:], phase, -1, section)
    return [piece, from_right, from_left, upper, lower]


def direct_reduce(blocks, phase, section):
    place = ring_place(phase)

    def block(steps):
        return lax.dynamic_index_in_dim(blocks, (place + steps) % SIDE, 1, keepdims=False)

    taken = [along(block(steps), phase, steps, section) for steps in (1, 2, 3)]
    return added(block(0), *taken)


def direct_parts(piece, phase, section):
    return [piece] + [along(piece, phase, -steps, section) for steps in (1, 2, 3)]


def plane_reduce(pieces, section):
    groups, count, rows, width = pieces.shape
    blocks = ring_reduce(pieces.reshape(groups, SIDE, SIDE * rows, width), 0, section)
    return direct_reduce(blocks.reshape(groups, SIDE, rows, width), 1, section)


def plane_gather(first, second, section):
    count, rest, width = first.shape[0], second.shape[0], first.shape[1]
    parts = direct_parts(jnp.concatenate([first, second]), 1, section)
    place = ring_place(1)
    (block,) = unwritten(jax.ShapeDtypeStruct((SIDE * (count + rest), width), first.dtype))
    for steps, part in enumerate(parts):
        at = (place + steps) % SIDE
        block = lax.dynamic_update_slice(block, part[:count], (at * count, 0))
        block = lax.dynamic_update_slice(block, part[count:], (SIDE * count + at * rest, 0))
    half = SIDE * count
    own, after, before, upper, lower = ring_pieces(block, 0, section, half)
    wholes = (own, after, before)
    firsts = [part[:half] for part in wholes] + [upper]
    seconds = [part[half:] for part in wholes] + [lower]
    return (
        [part.reshape(SIDE, count, width) for part in firsts],
        [part.reshape(SIDE, rest, width) for part in seconds],
    )


def in_place_order(blocks):
    place = ring_place(0)
    (whole,) = unwritten(jax.ShapeDtypeStruct((SIDE,) + blocks[0].shape, blocks[0].dtype))
    for steps, block in zip((0, 1, 3, 2), blocks):
        whole = lax.dynamic_update_index_in_dim(whole, block, (place + steps) % SIDE, 0)
    return whole


def spread(piece):
    return lax.all_to_all(jnp.tile(piece, (SIDE * SIDE, 1)), "dp", 0, 0, tiled=True)


def summed_piece(pieces):
    taken = lax.all_to_all(pieces, "dp", 0, 0, tiled=True)
    return jnp.sum(taken.astype(F32), axis=0).astype(BF)


CUTS = (0, 144, 192, 384, 416)


def gathered(quarters, down, section):
    share = lax.dynamic_index_in_dim(quarters, ring_place(0), 0, keepdims=False)
    taken = to_chip(share, section)
    own_core = (to_core(quarters, section), to_core(down, section))
    own_core, taken, later = lax.optimization_barrier((own_core, taken, down))
    other_down = to_chip(later, section)
    own, after, before, upper, lower = ring_pieces(taken, 0, section)
    place = ring_place(0)
    other = jnp.zeros(quarters.shape, quarters.dtype)
    for steps, part in ((0, own), (1, after), (3, before)):
        other = lax.dynamic_update_index_in_dim(other, part, (place + steps) % SIDE, 0)
    other = lax.dynamic_update_slice(other, upper[None], ((place + 2) % SIDE, 0, 0))
    other = lax.dynamic_update_slice(other, lower[None], ((place + 2) % SIDE, upper.shape[0], 0))
    other_down, other = lax.optimization_barrier((other_down, other))
    return (*own_core, other, other_down, to_core(other, section), to_core(other_down, section))


def dot(left, right):
    return jnp.dot(left, right, preferred_element_type=F32)


def dot_t(left, right):
    return lax.dot_general(left, right, (((1,), (1,)), ((), ())), preferred_element_type=F32)


def t_dot(left, right):
    return lax.dot_general(left, right, (((0,), (0,)), ((), ())), preferred_element_type=F32)


def normalized(values):
    centered = values - jnp.mean(values, axis=-1, keepdims=True)
    spread = jnp.mean(centered * centered, axis=-1, keepdims=True)
    scale = lax.rsqrt(spread + EPSILON)
    return (centered * scale, scale)


def norm_backward(grad, values, gain):
    unit, scale = normalized(values)
    inner = grad * gain
    drop = jnp.mean(inner, axis=-1, keepdims=True)
    slope = jnp.mean(inner * unit, axis=-1, keepdims=True)
    return (
        scale * (inner - drop - unit * slope),
        jnp.sum(grad * unit, axis=0),
        jnp.sum(grad, axis=0),
    )


SLOPE = 0.7978845608028654
CUBIC = 0.044715


def one_hot(indices, names):
    return (indices[..., None] == names).astype(BF)


def heads_of(mixed):
    shaped = mixed.reshape(-1, TILE, mixed.shape[1] // 576, 3, 3, HEAD_DIM)
    return [shaped[:, :, :, part].reshape(-1, TILE, mixed.shape[1] // 192, HEAD_DIM) for part in range(3)]


def shares_of(q, k, marks):
    group, order = marks[:, 0].reshape(-1, TILE), marks[:, 1].reshape(-1, TILE)
    allowed = (group[:, :, None] == group[:, None, :]) & (order[:, None, :] <= order[:, :, None])
    scores = jnp.einsum("tqhe,tkhe->thqk", q, k, preferred_element_type=F32) * HEAD_DIM**-0.5
    scores = jnp.where(allowed[:, None], scores, -1e30)
    raised = jnp.exp(scores - jnp.max(scores, axis=-1, keepdims=True))
    return raised / jnp.sum(raised, axis=-1, keepdims=True)


def attend(mixed, marks):
    q, k, v = heads_of(mixed)
    shares = shares_of(q, k, marks)
    mixture = jnp.einsum("thqk,tkhe->tqhe", shares.astype(BF), v, preferred_element_type=F32)
    return (mixture.astype(BF).reshape(mixed.shape[0], -1), shares)


def attend_back(mixed, shares, grad):
    q, k, v = heads_of(mixed)
    scale = HEAD_DIM**-0.5
    grad = grad.reshape(q.shape)
    slopes = jnp.einsum("tqhe,tkhe->thqk", grad, v, preferred_element_type=F32)
    scores = (shares * (slopes - jnp.sum(shares * slopes, axis=-1, keepdims=True))).astype(BF)
    grads = [
        jnp.einsum("thqk,tkhe->tqhe", scores, k, preferred_element_type=F32) * scale,
        jnp.einsum("thqk,tqhe->tkhe", scores, q, preferred_element_type=F32) * scale,
        jnp.einsum("thqk,tqhe->tkhe", shares.astype(BF), grad, preferred_element_type=F32),
    ]
    shape = (mixed.shape[0], mixed.shape[1] // 576, 1, 192)
    return jnp.concatenate([part.astype(BF).reshape(shape) for part in grads], axis=2).reshape(mixed.shape)


def gelu_pair(upper):
    square = upper * upper
    bend = jnp.tanh(SLOPE * upper * (1.0 + CUBIC * square))
    near = 0.5 * (1.0 + bend)
    slope = near + 0.5 * SLOPE * upper * (1.0 - bend * bend) * (1.0 + 3 * CUBIC * square)
    return ((upper * near).astype(BF), slope)


def local_layer(rows, grad_result, weights, gains, marks):
    qkv_t, out, up_t, down, up_bias = weights
    unit, scale = normalized(rows)
    normed = (unit * gains[0] + gains[1]).astype(BF)
    mixed = dot_t(normed, qkv_t).astype(BF)
    mixture, shares = attend(mixed, marks)
    middle = rows + dot(mixture, out)
    normed_mlp = (normalized(middle)[0] * gains[2] + gains[3]).astype(BF)
    active, slope = gelu_pair(dot_t(normed_mlp, up_t) + up_bias)
    result = (middle + dot(active, down) + gains[4]).astype(BF)
    grad_branch = grad_result.astype(BF)
    grad_upper = (slope * dot_t(grad_branch, down)).astype(BF)
    from_norm, *mlp_sums = norm_backward(dot(grad_upper, up_t), middle, gains[2])
    grad_middle = grad_result + from_norm
    grad_middle_low = grad_middle.astype(BF)
    grad_mixed = attend_back(mixed, shares, dot_t(grad_middle_low, out).astype(BF))
    from_norm, *attn_sums = norm_backward(dot(grad_mixed, qkv_t), rows, gains[0])
    grad_rows = (grad_middle + from_norm).astype(BF)
    sums = attn_sums + mlp_sums + [jnp.sum(grad_branch.astype(F32), axis=0)]
    vectors = jnp.concatenate([jnp.stack(sums), jnp.zeros((3, WIDTH), F32)])
    up_sums = jnp.sum(grad_upper.astype(F32), axis=0)
    stored = (normed, mixture, normed_mlp, active, grad_branch, grad_upper, grad_middle_low, grad_mixed)
    return (result, grad_rows, stored, vectors, up_sums)


def placed_bytes(mine, theirs, chip, core):
    rows, width = mine[0].shape[1] // 4, mine[0].shape[2]
    whole = jnp.zeros((8, SIDE, SIDE * rows, width), F32)
    for blocks, of_core, place in ((mine, core, ring_place(0)), (theirs, 1 - core, ring_place(1))):
        for steps, block in zip((0, 1, 3, 2), blocks):
            parts = block.reshape(SIDE, 2, 2, rows, width)
            for chips in range(2):
                part = jnp.swapaxes(parts[:, chips], 0, 1).reshape(2, 1, SIDE * rows, width)
                at = 4 * (chip ^ chips) + 2 * of_core
                whole = lax.dynamic_update_slice(
                    whole, part.astype(F32), (at, (place + steps) % SIDE, 0, 0)
                )
    return whole


def local(
    tokens,
    doc_lengths,
    byte_embed,
    patch_maps,
    attn_gain,
    attn_shift,
    qkv_weight,
    out_weight,
    mlp_gain,
    mlp_shift,
    up_weight,
    up_bias,
    down_weight,
    down_bias,
    cotangent,
):
    packs = tokens.shape[0]
    patches = tokens.shape[1] // PATCH
    own = patches // 4
    own_rows = packs * own
    rank = lax.axis_index("tensor")
    chip, core = rank // 2, rank % 2
    first_section = lax.axis_index("section") == 0
    embed, mapping = byte_embed[0], patch_maps[0]
    ranks = [rank ^ mask for mask in RELATIVE]
    gains = (attn_gain[0], attn_shift[0], mlp_gain[0], mlp_shift[0], down_bias[0])
    qkv_t = qkv_weight[0].reshape(WIDTH, 576).T
    up_t = up_weight[0].T
    out, down = out_weight[0], down_weight[0]

    places = jnp.arange(tokens.shape[1], dtype=jnp.int32)
    ends = jnp.cumsum(doc_lengths, axis=1)
    docs = jnp.sum((ends[:, None, :] <= places[None, :, None]).astype(jnp.int32), axis=2)
    names = jnp.arange(VOCAB, dtype=jnp.int32)

    def by_rank(values):
        quarters = values.reshape((packs, 4, own) + values.shape[2:])
        return jnp.stack(
            [lax.dynamic_index_in_dim(quarters, r, 1, keepdims=False) for r in ranks], axis=1
        )

    def to_own(partial):
        blocks = partial.astype(BF).reshape(packs, 4, own, WIDTH)
        pair = added(blocks[:, :2], to_core(blocks[:, 2:], 0))
        mine = pair[:, 0].astype(F32) + to_chip(pair[:, 1], 0).astype(F32)
        return mine.reshape(own_rows, WIDTH)

    def to_all(partial):
        blocks = partial.astype(BF).reshape(packs, 2, 2, own, WIDTH)
        pair = added(blocks, to_core(blocks, 0)[:, ::-1])
        whole = pair.astype(F32) + to_chip(pair, 0)[:, :, ::-1].astype(F32)
        return whole.reshape(-1, WIDTH)

    grouped = tokens.reshape(packs, patches, PATCH)
    before = jnp.concatenate([jnp.full((packs, 1, PATCH), -1, jnp.int32), grouped[:, :-1]], axis=1)
    before = by_rank(before).reshape(packs * patches, PATCH).T
    patch_rank = by_rank(jnp.broadcast_to(jnp.arange(patches, dtype=jnp.int32), (packs, patches)))
    global_marks = jnp.stack(
        [by_rank(docs[:, ::PATCH]).reshape(-1), patch_rank.reshape(-1)], axis=1
    )

    def mine_of(rows):
        return rows.reshape(packs, 4, own, -1)[:, 0].reshape(own_rows, -1)

    def global_pass():
        picked = one_hot(before, names)
        embedded = dot(picked.reshape(-1, VOCAB), embed).astype(BF).reshape(PATCH, -1, WIDTH)
        global_in = dot(jnp.concatenate(list(embedded), axis=1), mapping)
        normed = (normalized(global_in)[0] * gains[0] + gains[1]).astype(BF)
        mixed = dot_t(normed, qkv_t).astype(BF)
        mixture, shares = attend(mixed, global_marks)
        middle = global_in + to_all(dot(mixture, out))
        normed_mlp = (normalized(middle)[0] * gains[2] + gains[3]).astype(BF)
        active, slope = gelu_pair(dot_t(normed_mlp, up_t) + up_bias)
        hidden = (mine_of(middle) + to_own(dot(active, down)) + gains[4]).astype(BF)
        return (hidden, (global_in, normed, mixed, mixture, middle, normed_mlp, slope, active, shares))

    def weights_of_all():
        bias_high = up_bias.astype(BF)
        bias_rest = up_bias - bias_high.astype(F32)
        bias_middle = bias_rest.astype(BF)
        bias_low = (bias_rest - bias_middle.astype(F32)).astype(BF)
        bias_rows = jnp.pad(jnp.concatenate([bias_high, bias_middle, bias_low]), ((0, 29), (0, 0)))
        quarters = jnp.concatenate(
            [
                qkv_t.reshape(4, 144, WIDTH),
                out.reshape(4, 48, WIDTH),
                up_t.reshape(4, 192, WIDTH),
                jnp.broadcast_to(bias_rows[None], (4, 32, WIDTH)),
            ],
            axis=1,
        )
        return gathered(quarters, down, 1)

    def in_first():
        return global_pass() + (unwritten(*jax.eval_shape(weights_of_all)),)

    def in_second():
        first, rest = jax.eval_shape(global_pass)
        return (jnp.zeros(first.shape, first.dtype), tuple(unwritten(*rest)), list(weights_of_all()))

    hidden, global_stored, full = lax.cond(first_section, in_first, in_second)
    arrived = send(hidden, lambda y, z, s, t: (y, z, 1, t), (0,))
    global_out = jnp.where(first_section, hidden, arrived).reshape(packs, own, WIDTH)

    own_bytes = own * PATCH
    own_tokens = lax.dynamic_slice_in_dim(tokens, rank * own_bytes, own_bytes, 1)
    own_docs = lax.dynamic_slice_in_dim(docs, rank * own_bytes, own_bytes, 1)
    spot = jnp.arange(own_bytes, dtype=jnp.int32)
    earlier = jnp.where(spot % PATCH == 0, -1, jnp.roll(own_tokens, 1, axis=1)).reshape(-1, 1)
    group = (spot // PATCH) * 16 + own_docs
    rank_in = jnp.broadcast_to(spot % PATCH, group.shape)
    local_marks = jnp.stack([group.reshape(-1), rank_in.reshape(-1)], axis=1)
    core_rows, core_down, other_rows, other_down, other_core_rows, other_core_down = full
    others = (other_rows, core_rows, other_core_rows)

    def family(own_part, at):
        parts = [rows[:, CUTS[at] : CUTS[at + 1]].reshape(own_part.shape) for rows in others]
        return jnp.concatenate([own_part] + parts)

    bias = jnp.concatenate(
        [up_bias]
        + [jnp.sum(rows[0, CUTS[3] : CUTS[3] + 3].astype(F32), axis=0, keepdims=True) for rows in others],
        axis=1,
    )
    weights = (
        family(qkv_t, 0),
        family(out, 1),
        family(up_t, 2),
        jnp.concatenate([down, other_down, core_down, other_core_down]),
        bias,
    )
    stream = dot_t(arrived, mapping).reshape(-1, WIDTH)
    local_in = stream + dot(one_hot(earlier[:, 0], names), embed)
    result_low, grad_rows, stored, vectors, up_sums = local_layer(
        local_in, cotangent.reshape(-1, WIDTH), weights, gains, local_marks
    )
    grad_hidden = dot(grad_rows.reshape(own_rows, PATCH * WIDTH), mapping).astype(BF)
    half_width = WIDTH // 2
    halves = result_low.reshape(packs, own_bytes, WIDTH)
    message = jnp.concatenate([halves[0, :, :half_width], halves[1, :, :half_width]], axis=1)
    message = jnp.concatenate([grad_hidden, message])
    given = send(message, lambda y, z, s, t: (y, z, 0, t), (1,))
    returned = [given[:own_rows]] + [
        send(grad_hidden, lambda y, z, s, t, mask=mask: (y, z, 0, t ^ mask), (1,))
        for mask in RELATIVE[1:]
    ]
    both_halves = jnp.stack([given[own_rows:, :half_width], given[own_rows:, half_width:]])
    local_out = jnp.where(first_section, both_halves, halves[..., half_width:])
    grad_bytes = jnp.swapaxes(grad_rows.reshape(own_rows, PATCH, WIDTH), 0, 1)
    normed, mixture, normed_mlp, active, grad_branch, grad_upper, grad_middle_low, grad_mixed = stored

    by_byte = grad_bytes.reshape(4, 2, own_rows, WIDTH)

    def bytes_of(mask):
        part = lax.dynamic_index_in_dim(by_byte, rank ^ mask, 0, keepdims=False)
        return jnp.concatenate([part, arrived[None]])

    shares = [
        send(bytes_of(mask), lambda y, z, s, t, mask=mask: (y, z, s, t ^ mask), (1,))
        if mask
        else bytes_of(mask)
        for mask in RELATIVE
    ]

    def shaped_out(grad_qkv, grad_out, grad_up, grad_down, small, grad_embed, grad_map):
        small = small.astype(F32)
        return (
            grad_embed[None],
            grad_map.reshape(1, -1, WIDTH),
            small[0][None],
            small[1][None],
            grad_qkv.T.astype(F32).reshape(1, WIDTH, 3, 192),
            grad_out.astype(F32)[None],
            small[2][None],
            small[3][None],
            grad_up.T.astype(F32)[None],
            small[5][None],
            grad_down.astype(F32)[None],
            small[4][None],
        )

    def global_tail():
        global_in, normed, mixed, mixture, middle, normed_mlp, slope, active, shares = global_stored
        grad_branch = jnp.stack(returned).reshape(4, packs, own, WIDTH).swapaxes(0, 1)
        grad_branch = grad_branch.reshape(-1, WIDTH)
        grad_upper = (slope * dot_t(grad_branch, down)).astype(BF)
        grad_up = t_dot(grad_upper, normed_mlp).astype(BF)
        grad_down = t_dot(active, grad_branch).astype(BF)
        from_norm, *mlp_sums = norm_backward(to_all(dot(grad_upper, up_t)), middle, gains[2])
        grad_middle = grad_branch.astype(F32) + from_norm
        grad_middle_low = grad_middle.astype(BF)
        grad_mixture = dot_t(grad_middle_low, out).astype(BF)
        grad_mixed = attend_back(mixed, shares, grad_mixture)
        from_norm, *attn_sums = norm_backward(to_all(dot(grad_mixed, qkv_t)), global_in, gains[0])
        grad_in = (grad_middle + from_norm).astype(BF)
        positions = lax.dynamic_slice_in_dim(before, rank * 2, 2, 0)
        counts = jnp.einsum(
            "jrv,rd->jvd", one_hot(positions, names), grad_in, preferred_element_type=F32
        ).astype(BF)
        small = jnp.stack(
            attn_sums
            + mlp_sums
            + [jnp.sum(grad_branch.astype(F32), axis=0), jnp.sum(grad_upper.astype(F32), axis=0)]
        )
        attn = jnp.concatenate(
            [t_dot(grad_mixed, normed).astype(BF), t_dot(mixture, grad_middle_low).astype(BF)]
        )
        pieces = jnp.concatenate(
            [
                grad_up.reshape(16, 48, WIDTH),
                grad_down.reshape(16, 48, WIDTH),
                attn.reshape(16, 48, WIDTH),
                jnp.pad(small, ((0, 122), (0, 0))).astype(BF).reshape(16, 8, WIDTH),
                jnp.swapaxes(counts.reshape(2, 16, 16, WIDTH), 0, 1).reshape(16, 32, WIDTH),
            ],
            axis=1,
        )
        piece = summed_piece(pieces)
        piece = jnp.concatenate([piece, to_chip(piece[152:], 0)])
        summed = spread(piece).reshape(16, 216, WIDTH)
        counts = jnp.swapaxes(summed[:, 152:].reshape(16, 4, 16, WIDTH), 0, 1).reshape(4, VOCAB, WIDTH)
        counts = in_order(counts, to_core(counts, 0))
        grad_up, grad_down, attn = [
            summed[:, start : start + 48].reshape(WIDTH, WIDTH) for start in (0, 48, 96)
        ]
        small = summed[0, 144:152]
        by_byte = mapping.reshape(PATCH, WIDTH, WIDTH)
        grad_map = jnp.einsum("vd,jve->jde", embed, counts, preferred_element_type=F32)
        grad_embed = jnp.einsum("jve,jde->vd", counts, by_byte, preferred_element_type=F32)
        return shaped_out(attn[:576], attn[576:], grad_up, grad_down, small, grad_embed, grad_map)

    def in_order(mine, theirs):
        shape = (2, 2) + mine.shape[1:]
        both = jnp.stack([mine.reshape(shape), theirs.reshape(shape)], axis=1)
        both = jnp.where(core == 0, both, both[:, ::-1])
        return jnp.where(chip == 0, both, both[::-1]).reshape((8,) + mine.shape[1:])

    def local_tail():
        products = (
            (grad_upper, normed_mlp),
            (active, grad_branch),
            (grad_mixed, normed),
            (mixture, grad_middle_low),
        )
        takens = [
            to_core(t_dot(left[:, left.shape[1] // 2 :], right).astype(BF), 1) for left, right in products
        ]
        embed_sums = t_dot(one_hot(earlier[:, 0], names), grad_rows).reshape(2, VOCAB // 2, WIDTH)
        ups = up_sums.reshape(2, 2, WIDTH)

        def half_with(half, up_sums):
            half = lax.dynamic_index_in_dim(embed_sums, half, 0, keepdims=False)
            return jnp.concatenate([half, vectors, up_sums, jnp.zeros((6, WIDTH), F32)])

        few_taken = to_core(half_with(1 - core, ups[1]).astype(BF), 1)

        both = jnp.pad(half_with(core, ups[0]) + few_taken.astype(F32), ((0, 112), (0, 0)))
        misc = jnp.stack([both, jnp.concatenate([both[:136], both[137:138], both[137:]])]).astype(BF)

        grad_up, grad_down, grad_qkv, grad_out = [
            added(t_dot(left[:, : left.shape[1] // 2], right), taken).reshape(2, -1, 48, WIDTH)
            for (left, right), taken in zip(products, takens)
        ]
        stacked = jnp.stack(shares)
        grad_map = jnp.einsum(
            "rkpd,rpe->kde", stacked[:, :2], stacked[:, 2], preferred_element_type=F32
        ).astype(BF)
        pieces = jnp.concatenate(
            [
                grad_up,
                grad_down,
                jnp.concatenate([grad_qkv, grad_out], axis=1),
                misc.reshape(2, 16, 16, WIDTH),
                grad_map.reshape(2, 16, 48, WIDTH),
            ],
            axis=2,
        )
        piece = plane_reduce(pieces, 1)
        taken = to_chip(jnp.concatenate([piece[1, :160], piece[0, 160:], piece[1, 160:]]), 1)
        piece = jnp.concatenate(
            [added(piece[0, :160], taken[:160]), piece[0, 160:], piece[1, 160:], taken[160:]]
        )
        maps, rows = plane_gather(piece[160:], piece[:160], 1)
        grad_map = placed_bytes(maps, [to_core(part, 1) for part in maps], chip, core)
        summed = in_place_order(rows).reshape(16, 160, WIDTH)
        grad_up, grad_down, attn = [
            summed[:, start : start + 48].reshape(WIDTH, WIDTH) for start in (0, 48, 96)
        ]
        misc = summed[:, 144:160].reshape(256, WIDTH)
        grad_embed, other = misc[:128], to_core(misc[:128], 1)
        grad_embed = jnp.concatenate(
            [jnp.where(core == 0, grad_embed, other), jnp.where(core == 0, other, grad_embed)]
        ).astype(F32)
        small = jnp.concatenate([misc[128:133], misc[136:137]])
        return shaped_out(attn[:576], attn[576:], grad_up, grad_down, small, grad_embed, grad_map)

    return (global_out, local_out) + lax.cond(first_section, global_tail, local_tail)


def solution(mesh):
    placed = (
        P("dp", None),
        P("dp", None),
        P("section", None, None),
        P("section", None, None),
        P("section", None),
        P("section", None),
        P("section", None, None, "tensor"),
        P("section", "tensor", None),
        P("section", None),
        P("section", None),
        P("section", None, "tensor"),
        P("section", "tensor"),
        P("section", "tensor", None),
        P("section", None),
        P("dp", "tensor", None),
    )
    return jax.shard_map(
        local,
        mesh=mesh,
        in_specs=placed,
        out_specs=(
            P("dp", "tensor", None),
            P("dp", "tensor", "section"),
            P("section", None, None),
            P("section", None, None),
            P("section", None),
            P("section", None),
            P("section", None, None, "tensor"),
            P("section", "tensor", None),
            P("section", None),
            P("section", None),
            P("section", None, "tensor"),
            P("section", "tensor"),
            P("section", "tensor", None),
            P("section", None),
        ),
        check_vma=False,
    )
```

```python
from functools import partial

import jax
import jax.numpy as jnp
from jax import lax
from jax.sharding import PartitionSpec as P

HEAD_DIM = 64
PATCH = 8
WIDTH = 768
VOCAB = 256
EPSILON = 1e-05
SIDE = 4
TILE = 128
RELATIVE = (0, 2, 1, 3)
BF = jnp.bfloat16
F32 = jnp.float32


def send(value, move, sections=(0, 1)):
    def flat(y, z, s, t):
        return ((y % SIDE * SIDE + z % SIDE) * 2 + s) * 4 + t

    pairs = [
        (flat(y, z, s, t), flat(*move(y, z, s, t)))
        for y in range(SIDE)
        for z in range(SIDE)
        for s in sections
        for t in range(4)
    ]
    return lax.ppermute(value, ("dp", "section", "tensor"), pairs)


def to_core(value, section):
    return send(value, lambda y, z, s, t: (y, z, s, t ^ 1), (section,))


def to_chip(value, section):
    return send(value, lambda y, z, s, t: (y, z, s, t ^ 2), (section,))


def along(value, phase, step, section):
    def move(y, z, s, t):
        return (y + step, z, s, t) if t % 2 == phase else (y, z + step, s, t)

    return send(value, move, (section,))


def ring_place(phase):
    place = lax.axis_index("dp")
    core = lax.axis_index("tensor") % 2
    return jnp.where(core == phase, place // SIDE, place % SIDE)


def added(*parts):
    total = parts[0].astype(F32)
    for part in parts[1:]:
        total = total + part.astype(F32)
    return total.astype(BF)


def half_of(count):
    return (count // 2 + 7) // 8 * 8


def unwritten(*shapes):
    return [jnp.zeros(shape.shape, shape.dtype) for shape in shapes]


def ring_reduce(blocks, phase, section):
    place = ring_place(phase)
    half = half_of(blocks.shape[2])

    def block(steps):
        return lax.dynamic_index_in_dim(blocks, (place + steps) % SIDE, 1, keepdims=False)

    far, right, left = block(2), block(1), block(3)
    upper = along(far[:, :half], phase, 1, section)
    lower = along(far[:, half:], phase, -1, section)
    right = jnp.concatenate([added(right[:, :half], upper), right[:, half:]], axis=1)
    left = jnp.concatenate([left[:, :half], added(left[:, half:], lower)], axis=1)
    from_left = along(right, phase, 1, section)
    from_right = along(left, phase, -1, section)
    return added(block(0), from_left, from_right)


def ring_pieces(piece, phase, section, half=None):
    half = half or half_of(piece.shape[0])
    from_left = along(piece, phase, 1, section)
    from_right = along(piece, phase, -1, section)
    upper = along(from_left[:half], phase, 1, section)
    lower = along(from_right[half:], phase, -1, section)
    return [piece, from_right, from_left, upper, lower]


def direct_reduce(blocks, phase, section):
    place = ring_place(phase)

    def block(steps):
        return lax.dynamic_index_in_dim(blocks, (place + steps) % SIDE, 1, keepdims=False)

    taken = [along(block(steps), phase, steps, section) for steps in (1, 2, 3)]
    return added(block(0), *taken)


def direct_parts(piece, phase, section):
    return [piece] + [along(piece, phase, -steps, section) for steps in (1, 2, 3)]


def plane_reduce(pieces, section):
    groups, count, rows, width = pieces.shape
    blocks = ring_reduce(pieces.reshape(groups, SIDE, SIDE * rows, width), 0, section)
    return direct_reduce(blocks.reshape(groups, SIDE, rows, width), 1, section)


def plane_gather(first, second, section):
    count, rest, width = first.shape[0], second.shape[0], first.shape[1]
    parts = direct_parts(jnp.concatenate([first, second]), 1, section)
    place = ring_place(1)
    (block,) = unwritten(jax.ShapeDtypeStruct((SIDE * (count + rest), width), first.dtype))
    for steps, part in enumerate(parts):
        at = (place + steps) % SIDE
        block = lax.dynamic_update_slice(block, part[:count], (at * count, 0))
        block = lax.dynamic_update_slice(block, part[count:], (SIDE * count + at * rest, 0))
    half = SIDE * count
    own, after, before, upper, lower = ring_pieces(block, 0, section, half)
    wholes = (own, after, before)
    firsts = [part[:half] for part in wholes] + [upper]
    seconds = [part[half:] for part in wholes] + [lower]
    return (
        [part.reshape(SIDE, count, width) for part in firsts],
        [part.reshape(SIDE, rest, width) for part in seconds],
    )


def in_place_order(blocks):
    place = ring_place(0)
    (whole,) = unwritten(jax.ShapeDtypeStruct((SIDE,) + blocks[0].shape, blocks[0].dtype))
    for steps, block in zip((0, 1, 3, 2), blocks):
        whole = lax.dynamic_update_index_in_dim(whole, block, (place + steps) % SIDE, 0)
    return whole


def spread(piece):
    return lax.all_to_all(jnp.tile(piece, (SIDE * SIDE, 1)), "dp", 0, 0, tiled=True)


def summed_piece(pieces):
    taken = lax.all_to_all(pieces, "dp", 0, 0, tiled=True)
    return jnp.sum(taken.astype(F32), axis=0).astype(BF)


CUTS = (0, 576, 768, 1536, 1664)


def gathered(quarters, down, section):
    share = lax.dynamic_index_in_dim(quarters, ring_place(0), 0, keepdims=False)
    taken = to_chip(share, section)
    own_core = (to_core(quarters, section), to_core(down, section))
    own_core, taken, later = lax.optimization_barrier((own_core, taken, down))
    other_down = to_chip(later, section)
    own, after, before, upper, lower = ring_pieces(taken, 0, section)
    place = ring_place(0)
    other = jnp.zeros(quarters.shape, quarters.dtype)
    for steps, part in ((0, own), (1, after), (3, before)):
        other = lax.dynamic_update_index_in_dim(other, part, (place + steps) % SIDE, 0)
    other = lax.dynamic_update_slice(other, upper[None], ((place + 2) % SIDE, 0, 0))
    other = lax.dynamic_update_slice(other, lower[None], ((place + 2) % SIDE, upper.shape[0], 0))
    other_down, other = lax.optimization_barrier((other_down, other))
    return (*own_core, other, other_down, to_core(other, section), to_core(other_down, section))


def dot(left, right):
    return jnp.dot(left, right, preferred_element_type=F32)


def dot_t(left, right):
    return lax.dot_general(left, right, (((1,), (1,)), ((), ())), preferred_element_type=F32)


def t_dot(left, right):
    return lax.dot_general(left, right, (((0,), (0,)), ((), ())), preferred_element_type=F32)


def normalized(values):
    centered = values - jnp.mean(values, axis=-1, keepdims=True)
    spread = jnp.mean(centered * centered, axis=-1, keepdims=True)
    scale = lax.rsqrt(spread + EPSILON)
    return (centered * scale, scale)


def norm_backward(grad, values, gain):
    unit, scale = normalized(values)
    inner = grad * gain
    drop = jnp.mean(inner, axis=-1, keepdims=True)
    slope = jnp.mean(inner * unit, axis=-1, keepdims=True)
    return (
        scale * (inner - drop - unit * slope),
        jnp.sum(grad * unit, axis=0),
        jnp.sum(grad, axis=0),
    )


SLOPE = 0.7978845608028654
CUBIC = 0.044715


def one_hot(indices, names):
    return (indices[..., None] == names).astype(BF)


def by_tile(wide):
    return jnp.stack([wide[:, at : at + TILE] for at in range(0, wide.shape[1], TILE)])


def from_tiles(tiled):
    return jnp.concatenate(list(tiled), axis=1)


def heads_of(mixed):
    shaped = mixed.reshape(mixed.shape[0], -1, 3, 3, HEAD_DIM, TILE)
    return [shaped[:, :, part] for part in range(3)]


def attend(mixed, marks):
    q, k, v = heads_of(mixed)
    group, order = marks[:, 0].reshape(-1, TILE), marks[:, 1].reshape(-1, TILE)
    allowed = (group[:, :, None] == group[:, None, :]) & (order[:, None, :] <= order[:, :, None])
    scores = jnp.einsum("tsheq,tshek->tshqk", q, k, preferred_element_type=F32) * HEAD_DIM**-0.5
    scores = jnp.where(allowed[:, None, None], scores, -1e30)
    raised = jnp.exp(scores - jnp.max(scores, axis=-1, keepdims=True))
    shares = raised / jnp.sum(raised, axis=-1, keepdims=True)
    mixture = jnp.einsum("tshqk,tshek->tsheq", shares.astype(BF), v, preferred_element_type=F32)
    return (from_tiles(mixture.astype(BF).reshape(mixed.shape[0], -1, TILE)), shares)


def attend_back(mixed, shares, grad):
    q, k, v = heads_of(mixed)
    scale = HEAD_DIM**-0.5
    grad = by_tile(grad).reshape(q.shape)
    slopes = jnp.einsum("tsheq,tshek->tshqk", grad, v, preferred_element_type=F32)
    scores = (shares * (slopes - jnp.sum(shares * slopes, axis=-1, keepdims=True))).astype(BF)
    grads = [
        jnp.einsum("tshqk,tshek->tsheq", scores, k, preferred_element_type=F32) * scale,
        jnp.einsum("tshqk,tsheq->tshek", scores, q, preferred_element_type=F32) * scale,
        jnp.einsum("tshqk,tsheq->tshek", shares.astype(BF), grad, preferred_element_type=F32),
    ]
    return from_tiles(jnp.stack([part.astype(BF) for part in grads], axis=2).reshape(mixed.shape))


def gelu_pair(upper):
    upper = lax.optimization_barrier(upper)
    square = upper * upper
    bend = jnp.tanh(SLOPE * upper * (1.0 + CUBIC * square))
    near = 0.5 * (1.0 + bend)
    slope = near + 0.5 * SLOPE * upper * (1.0 - bend * bend) * (1.0 + 3 * CUBIC * square)
    return lax.optimization_barrier(((upper * near).astype(BF), slope))


def local_layer(rows, grad_result, weights, gains, marks):
    qkv_t, out, up_t, down, up_bias = weights
    unit, scale = normalized(rows)
    normed = (unit * gains[0] + gains[1]).astype(BF)
    mixed = by_tile(dot_t(qkv_t, normed).astype(BF))
    mixture, shares = attend(mixed, marks)
    middle = rows + t_dot(mixture, out)
    normed_mlp = (normalized(middle)[0] * gains[2] + gains[3]).astype(BF)
    active, slope = gelu_pair(dot_t(normed_mlp, up_t) + up_bias)
    result = (middle + dot(active, down) + gains[4]).astype(BF)
    grad_branch = grad_result.astype(BF)
    grad_upper = (slope * dot_t(grad_branch, down)).astype(BF)
    from_norm, *mlp_sums = norm_backward(dot(grad_upper, up_t), middle, gains[2])
    grad_middle = grad_result + from_norm
    grad_middle_low = grad_middle.astype(BF)
    grad_mixed = attend_back(mixed, shares, dot_t(out, grad_middle_low).astype(BF))
    from_norm, *attn_sums = norm_backward(t_dot(grad_mixed, qkv_t), rows, gains[0])
    grad_rows = (grad_middle + from_norm).astype(BF)
    sums = attn_sums + mlp_sums + [jnp.sum(grad_branch.astype(F32), axis=0)]
    vectors = jnp.concatenate([jnp.stack(sums), jnp.zeros((3, WIDTH), F32)])
    up_sums = jnp.sum(grad_upper.astype(F32), axis=0)
    stored = (normed, mixture, normed_mlp, active, grad_branch, grad_upper, grad_middle_low, grad_mixed)
    return (result, grad_rows, stored, vectors, up_sums)


def placed_bytes(mine, theirs, chip, core):
    rows, width = mine[0].shape[1] // 4, mine[0].shape[2]
    whole = jnp.zeros((8, SIDE, SIDE * rows, width), F32)
    for blocks, of_core, place in ((mine, core, ring_place(0)), (theirs, 1 - core, ring_place(1))):
        for steps, block in zip((0, 1, 3, 2), blocks):
            parts = block.reshape(SIDE, 2, 2, rows, width)
            for chips in range(2):
                part = jnp.swapaxes(parts[:, chips], 0, 1).reshape(2, 1, SIDE * rows, width)
                at = 4 * (chip ^ chips) + 2 * of_core
                whole = lax.dynamic_update_slice(
                    whole, part.astype(F32), (at, (place + steps) % SIDE, 0, 0)
                )
    return whole


def local(
    tokens,
    doc_lengths,
    byte_embed,
    patch_maps,
    attn_gain,
    attn_shift,
    qkv_weight,
    out_weight,
    mlp_gain,
    mlp_shift,
    up_weight,
    up_bias,
    down_weight,
    down_bias,
    cotangent,
):
    packs = tokens.shape[0]
    patches = tokens.shape[1] // PATCH
    own = patches // 4
    own_rows = packs * own
    rank = lax.axis_index("tensor")
    chip, core = rank // 2, rank % 2
    first_section = lax.axis_index("section") == 0
    embed, mapping = byte_embed[0], patch_maps[0]
    ranks = [rank ^ mask for mask in RELATIVE]
    gains = (attn_gain[0], attn_shift[0], mlp_gain[0], mlp_shift[0], down_bias[0])
    qkv_t = qkv_weight[0].reshape(WIDTH, 576).T
    up_t = up_weight[0].T
    out, down = out_weight[0], down_weight[0]

    places = jnp.arange(tokens.shape[1], dtype=jnp.int32)
    ends = jnp.cumsum(doc_lengths, axis=1)
    docs = jnp.sum((ends[:, None, :] <= places[None, :, None]).astype(jnp.int32), axis=2)
    names = jnp.arange(VOCAB, dtype=jnp.int32)

    def by_rank(values):
        quarters = values.reshape((packs, 4, own) + values.shape[2:])
        return jnp.stack(
            [lax.dynamic_index_in_dim(quarters, r, 1, keepdims=False) for r in ranks], axis=1
        )

    def to_own(partial):
        blocks = partial.astype(BF).reshape(packs, 4, own, WIDTH)
        pair = added(blocks[:, :2], to_core(blocks[:, 2:], 0))
        mine = pair[:, 0].astype(F32) + to_chip(pair[:, 1], 0).astype(F32)
        return mine.reshape(own_rows, WIDTH)

    def to_all(partial):
        blocks = partial.astype(BF).reshape(packs, 2, 2, own, WIDTH)
        pair = added(blocks, to_core(blocks, 0)[:, ::-1])
        whole = pair.astype(F32) + to_chip(pair, 0)[:, :, ::-1].astype(F32)
        return whole.reshape(-1, WIDTH)

    grouped = tokens.reshape(packs, patches, PATCH)
    before = jnp.concatenate([jnp.full((packs, 1, PATCH), -1, jnp.int32), grouped[:, :-1]], axis=1)
    before = by_rank(before).reshape(packs * patches, PATCH).T
    patch_rank = by_rank(jnp.broadcast_to(jnp.arange(patches, dtype=jnp.int32), (packs, patches)))
    global_marks = jnp.stack(
        [by_rank(docs[:, ::PATCH]).reshape(-1), patch_rank.reshape(-1)], axis=1
    )

    def mine_of(rows):
        return rows.reshape(packs, 4, own, -1)[:, 0].reshape(own_rows, -1)

    def global_pass():
        picked = one_hot(before, names)
        embedded = dot(picked.reshape(-1, VOCAB), embed).astype(BF).reshape(PATCH, -1, WIDTH)
        global_in = dot(jnp.concatenate(list(embedded), axis=1), mapping)
        normed = (normalized(global_in)[0] * gains[0] + gains[1]).astype(BF)
        mixed = by_tile(dot_t(qkv_t, normed).astype(BF))
        mixture, shares = attend(mixed, global_marks)
        middle = global_in + to_all(t_dot(mixture, out))
        normed_mlp = (normalized(middle)[0] * gains[2] + gains[3]).astype(BF)
        active, slope = gelu_pair(dot_t(normed_mlp, up_t) + up_bias)
        hidden = (mine_of(middle) + to_own(dot(active, down)) + gains[4]).astype(BF)
        return (hidden, (global_in, normed, mixed, mixture, middle, normed_mlp, slope, active, shares))

    def weights_of_all():
        bias_high = up_bias.astype(BF)
        bias_rest = up_bias - bias_high.astype(F32)
        bias_middle = bias_rest.astype(BF)
        bias_low = (bias_rest - bias_middle.astype(F32)).astype(BF)
        bias_rows = jnp.pad(jnp.concatenate([bias_high, bias_middle, bias_low]), ((0, 125), (0, 0)))
        quarters = jnp.concatenate([qkv_t, out, up_t, bias_rows]).reshape(4, -1, WIDTH)
        return gathered(quarters, down, 1)

    def in_first():
        return global_pass() + (unwritten(*jax.eval_shape(weights_of_all)),)

    def in_second():
        first, rest = jax.eval_shape(global_pass)
        return (jnp.zeros(first.shape, first.dtype), tuple(unwritten(*rest)), list(weights_of_all()))

    hidden, global_stored, full = lax.cond(first_section, in_first, in_second)
    arrived = send(hidden, lambda y, z, s, t: (y, z, 1, t), (0,))
    global_out = jnp.where(first_section, hidden, arrived).reshape(packs, own, WIDTH)

    own_bytes = own * PATCH
    own_tokens = lax.dynamic_slice_in_dim(tokens, rank * own_bytes, own_bytes, 1)
    own_docs = lax.dynamic_slice_in_dim(docs, rank * own_bytes, own_bytes, 1)
    spot = jnp.arange(own_bytes, dtype=jnp.int32)
    earlier = jnp.where(spot % PATCH == 0, -1, jnp.roll(own_tokens, 1, axis=1)).reshape(-1, 1)
    group = (spot // PATCH) * 16 + own_docs
    rank_in = jnp.broadcast_to(spot % PATCH, group.shape)
    local_marks = jnp.stack([group.reshape(-1), rank_in.reshape(-1)], axis=1)
    core_rows, core_down, other_rows, other_down, other_core_rows, other_core_down = full
    others = [rows.reshape(-1, WIDTH) for rows in (other_rows, core_rows, other_core_rows)]

    def family(own_part, at):
        return jnp.concatenate([own_part] + [rows[CUTS[at] : CUTS[at + 1]] for rows in others])

    bias = jnp.concatenate(
        [up_bias]
        + [jnp.sum(rows[CUTS[3] : CUTS[3] + 3].astype(F32), axis=0, keepdims=True) for rows in others],
        axis=1,
    )
    weights = (
        family(qkv_t, 0),
        family(out, 1),
        family(up_t, 2),
        jnp.concatenate([down, other_down, core_down, other_core_down]),
        bias,
    )
    stream = dot_t(arrived, mapping).reshape(-1, WIDTH)
    local_in = stream + dot(one_hot(earlier[:, 0], names), embed)
    result_low, grad_rows, stored, vectors, up_sums = local_layer(
        local_in, cotangent.reshape(-1, WIDTH), weights, gains, local_marks
    )
    grad_hidden = dot(grad_rows.reshape(own_rows, PATCH * WIDTH), mapping).astype(BF)
    half_width = WIDTH // 2
    halves = result_low.reshape(packs, own_bytes, WIDTH)
    message = jnp.concatenate([halves[0, :, :half_width], halves[1, :, :half_width]], axis=1)
    message = jnp.concatenate([grad_hidden, message])
    given = send(message, lambda y, z, s, t: (y, z, 0, t), (1,))
    returned = [given[:own_rows]] + [
        send(grad_hidden, lambda y, z, s, t, mask=mask: (y, z, 0, t ^ mask), (1,))
        for mask in RELATIVE[1:]
    ]
    both_halves = jnp.stack([given[own_rows:, :half_width], given[own_rows:, half_width:]])
    local_out = jnp.where(first_section, both_halves, halves[..., half_width:])
    grad_bytes = jnp.swapaxes(grad_rows.reshape(own_rows, PATCH, WIDTH), 0, 1)
    normed, mixture, normed_mlp, active, grad_branch, grad_upper, grad_middle_low, grad_mixed = stored

    by_byte = grad_bytes.reshape(4, 2, own_rows, WIDTH)

    def bytes_of(mask):
        part = lax.dynamic_index_in_dim(by_byte, rank ^ mask, 0, keepdims=False)
        return jnp.concatenate([part, arrived[None]])

    shares = [
        send(bytes_of(mask), lambda y, z, s, t, mask=mask: (y, z, s, t ^ mask), (1,))
        if mask
        else bytes_of(mask)
        for mask in RELATIVE
    ]

    def shaped_out(grad_qkv, grad_out, grad_up, grad_down, small, grad_embed, grad_map):
        small = small.astype(F32)
        return (
            grad_embed[None],
            grad_map.reshape(1, -1, WIDTH),
            small[0][None],
            small[1][None],
            grad_qkv.T.astype(F32).reshape(1, WIDTH, 3, 192),
            grad_out.astype(F32)[None],
            small[2][None],
            small[3][None],
            grad_up.T.astype(F32)[None],
            small[5][None],
            grad_down.astype(F32)[None],
            small[4][None],
        )

    def global_tail():
        global_in, normed, mixed, mixture, middle, normed_mlp, slope, active, shares = global_stored
        grad_branch = jnp.stack(returned).reshape(4, packs, own, WIDTH).swapaxes(0, 1)
        grad_branch = grad_branch.reshape(-1, WIDTH)
        grad_upper = (slope * dot_t(grad_branch, down)).astype(BF)
        grad_up = t_dot(grad_upper, normed_mlp).astype(BF)
        grad_down = t_dot(active, grad_branch).astype(BF)
        from_norm, *mlp_sums = norm_backward(to_all(dot(grad_upper, up_t)), middle, gains[2])
        grad_middle = grad_branch.astype(F32) + from_norm
        grad_middle_low = grad_middle.astype(BF)
        grad_mixture = dot_t(out, grad_middle_low).astype(BF)
        grad_mixed = attend_back(mixed, shares, grad_mixture)
        from_norm, *attn_sums = norm_backward(to_all(t_dot(grad_mixed, qkv_t)), global_in, gains[0])
        grad_in = (grad_middle + from_norm).astype(BF)
        positions = lax.dynamic_slice_in_dim(before, rank * 2, 2, 0)
        counts = jnp.einsum(
            "jrv,rd->jvd", one_hot(positions, names), grad_in, preferred_element_type=F32
        ).astype(BF)
        small = jnp.stack(
            attn_sums
            + mlp_sums
            + [jnp.sum(grad_branch.astype(F32), axis=0), jnp.sum(grad_upper.astype(F32), axis=0)]
        )
        attn = jnp.concatenate(
            [dot(grad_mixed, normed).astype(BF), dot(mixture, grad_middle_low).astype(BF)]
        )
        pieces = jnp.concatenate(
            [
                grad_up.reshape(16, 48, WIDTH),
                grad_down.reshape(16, 48, WIDTH),
                attn.reshape(16, 48, WIDTH),
                jnp.pad(small, ((0, 122), (0, 0))).astype(BF).reshape(16, 8, WIDTH),
                jnp.swapaxes(counts.reshape(2, 16, 16, WIDTH), 0, 1).reshape(16, 32, WIDTH),
            ],
            axis=1,
        )
        piece = summed_piece(pieces)
        piece = jnp.concatenate([piece, to_chip(piece[152:], 0)])
        summed = spread(piece).reshape(16, 216, WIDTH)
        counts = jnp.swapaxes(summed[:, 152:].reshape(16, 4, 16, WIDTH), 0, 1).reshape(4, VOCAB, WIDTH)
        counts = in_order(counts, to_core(counts, 0))
        grad_up, grad_down, attn = [
            summed[:, start : start + 48].reshape(WIDTH, WIDTH) for start in (0, 48, 96)
        ]
        small = summed[0, 144:152]
        by_byte = mapping.reshape(PATCH, WIDTH, WIDTH)
        grad_map = jnp.einsum("vd,jve->jde", embed, counts, preferred_element_type=F32)
        grad_embed = jnp.einsum("jve,jde->vd", counts, by_byte, preferred_element_type=F32)
        return shaped_out(attn[:576], attn[576:], grad_up, grad_down, small, grad_embed, grad_map)

    def in_order(mine, theirs):
        shape = (2, 2) + mine.shape[1:]
        both = jnp.stack([mine.reshape(shape), theirs.reshape(shape)], axis=1)
        both = jnp.where(core == 0, both, both[:, ::-1])
        return jnp.where(chip == 0, both, both[::-1]).reshape((8,) + mine.shape[1:])

    def local_tail():
        products = (
            (grad_upper, normed_mlp),
            (active, grad_branch),
            (grad_mixed, normed),
            (mixture, grad_middle_low),
        )
        def product(left, right, half):
            if left.shape[1] == right.shape[0]:
                size = left.shape[0] // 2
                return dot(left[half * size : (half + 1) * size], right)
            size = left.shape[1] // 2
            return t_dot(left[:, half * size : (half + 1) * size], right)

        takens = [to_core(product(left, right, 1).astype(BF), 1) for left, right in products]
        embed_sums = t_dot(one_hot(earlier[:, 0], names), grad_rows).reshape(2, VOCAB // 2, WIDTH)
        ups = up_sums.reshape(2, 2, WIDTH)

        def half_with(half, up_sums):
            half = lax.dynamic_index_in_dim(embed_sums, half, 0, keepdims=False)
            return jnp.concatenate([half, vectors, up_sums, jnp.zeros((6, WIDTH), F32)])

        few_taken = to_core(half_with(1 - core, ups[1]).astype(BF), 1)

        both = jnp.pad(half_with(core, ups[0]) + few_taken.astype(F32), ((0, 112), (0, 0)))
        misc = jnp.stack([both, jnp.concatenate([both[:136], both[137:138], both[137:]])]).astype(BF)

        grad_up, grad_down, grad_qkv, grad_out = [
            added(product(left, right, 0), taken).reshape(2, -1, 48, WIDTH)
            for (left, right), taken in zip(products, takens)
        ]
        stacked = jnp.stack(shares)
        grad_map = jnp.einsum(
            "rkpd,rpe->kde", stacked[:, :2], stacked[:, 2], preferred_element_type=F32
        ).astype(BF)
        pieces = jnp.concatenate(
            [
                grad_up,
                grad_down,
                jnp.concatenate([grad_qkv, grad_out], axis=1),
                misc.reshape(2, 16, 16, WIDTH),
                grad_map.reshape(2, 16, 48, WIDTH),
            ],
            axis=2,
        )
        piece = plane_reduce(pieces, 1)
        taken = to_chip(jnp.concatenate([piece[1, :160], piece[0, 160:], piece[1, 160:]]), 1)
        piece = jnp.concatenate(
            [added(piece[0, :160], taken[:160]), piece[0, 160:], piece[1, 160:], taken[160:]]
        )
        maps, rows = plane_gather(piece[160:], piece[:160], 1)
        grad_map = placed_bytes(maps, [to_core(part, 1) for part in maps], chip, core)
        summed = in_place_order(rows).reshape(16, 160, WIDTH)
        grad_up, grad_down, attn = [
            summed[:, start : start + 48].reshape(WIDTH, WIDTH) for start in (0, 48, 96)
        ]
        misc = summed[:, 144:160].reshape(256, WIDTH)
        grad_embed, other = misc[:128], to_core(misc[:128], 1)
        grad_embed = jnp.concatenate(
            [jnp.where(core == 0, grad_embed, other), jnp.where(core == 0, other, grad_embed)]
        ).astype(F32)
        small = jnp.concatenate([misc[128:133], misc[136:137]])
        return shaped_out(attn[:576], attn[576:], grad_up, grad_down, small, grad_embed, grad_map)

    return (global_out, local_out) + lax.cond(first_section, global_tail, local_tail)


def solution(mesh):
    placed = (
        P("dp", None),
        P("dp", None),
        P("section", None, None),
        P("section", None, None),
        P("section", None),
        P("section", None),
        P("section", None, None, "tensor"),
        P("section", "tensor", None),
        P("section", None),
        P("section", None),
        P("section", None, "tensor"),
        P("section", "tensor"),
        P("section", "tensor", None),
        P("section", None),
        P("dp", "tensor", None),
    )
    return jax.shard_map(
        local,
        mesh=mesh,
        in_specs=placed,
        out_specs=(
            P("dp", "tensor", None),
            P("dp", "tensor", "section"),
            P("section", None, None),
            P("section", None, None),
            P("section", None),
            P("section", None),
            P("section", None, None, "tensor"),
            P("section", "tensor", None),
            P("section", None),
            P("section", None),
            P("section", None, "tensor"),
            P("section", "tensor"),
            P("section", "tensor", None),
            P("section", None),
        ),
        check_vma=False,
    )
```

```python
from functools import partial

import jax
import jax.numpy as jnp
from jax import lax
from jax.sharding import PartitionSpec as P

HEAD_DIM = 64
PATCH = 8
WIDTH = 768
VOCAB = 256
EPSILON = 1e-05
SIDE = 4
TILE = 128
RELATIVE = (0, 2, 1, 3)
BF = jnp.bfloat16
F32 = jnp.float32


def send(value, move, sections=(0, 1)):
    def flat(y, z, s, t):
        return ((y % SIDE * SIDE + z % SIDE) * 2 + s) * 4 + t

    pairs = [
        (flat(y, z, s, t), flat(*move(y, z, s, t)))
        for y in range(SIDE)
        for z in range(SIDE)
        for s in sections
        for t in range(4)
    ]
    return lax.ppermute(value, ("dp", "section", "tensor"), pairs)


def to_core(value, section):
    return send(value, lambda y, z, s, t: (y, z, s, t ^ 1), (section,))


def to_chip(value, section):
    return send(value, lambda y, z, s, t: (y, z, s, t ^ 2), (section,))


def along(value, phase, step, section):
    def move(y, z, s, t):
        return (y + step, z, s, t) if t % 2 == phase else (y, z + step, s, t)

    return send(value, move, (section,))


def ring_place(phase):
    place = lax.axis_index("dp")
    core = lax.axis_index("tensor") % 2
    return jnp.where(core == phase, place // SIDE, place % SIDE)


def added(*parts):
    total = parts[0].astype(F32)
    for part in parts[1:]:
        total = total + part.astype(F32)
    return total.astype(BF)


def half_of(count):
    return (count // 2 + 7) // 8 * 8


def unwritten(*shapes):
    return [jnp.zeros(shape.shape, shape.dtype) for shape in shapes]


def ring_reduce(blocks, phase, section):
    place = ring_place(phase)
    half = half_of(blocks.shape[2])

    def block(steps):
        return lax.dynamic_index_in_dim(blocks, (place + steps) % SIDE, 1, keepdims=False)

    far, right, left = block(2), block(1), block(3)
    upper = along(far[:, :half], phase, 1, section)
    lower = along(far[:, half:], phase, -1, section)
    right = jnp.concatenate([added(right[:, :half], upper), right[:, half:]], axis=1)
    left = jnp.concatenate([left[:, :half], added(left[:, half:], lower)], axis=1)
    from_left = along(right, phase, 1, section)
    from_right = along(left, phase, -1, section)
    return added(block(0), from_left, from_right)


def ring_pieces(piece, phase, section, half=None):
    half = half or half_of(piece.shape[0])
    from_left = along(piece, phase, 1, section)
    from_right = along(piece, phase, -1, section)
    upper = along(from_left[:half], phase, 1, section)
    lower = along(from_right[half:], phase, -1, section)
    return [piece, from_right, from_left, upper, lower]


def direct_reduce(blocks, phase, section):
    place = ring_place(phase)

    def block(steps):
        return lax.dynamic_index_in_dim(blocks, (place + steps) % SIDE, 1, keepdims=False)

    taken = [along(block(steps), phase, steps, section) for steps in (1, 2, 3)]
    return added(block(0), *taken)


def direct_parts(piece, phase, section):
    return [piece] + [along(piece, phase, -steps, section) for steps in (1, 2, 3)]


def plane_reduce(pieces, section):
    groups, count, rows, width = pieces.shape
    blocks = ring_reduce(pieces.reshape(groups, SIDE, SIDE * rows, width), 0, section)
    return direct_reduce(blocks.reshape(groups, SIDE, rows, width), 1, section)


def plane_gather(first, second, section):
    count, rest, width = first.shape[0], second.shape[0], first.shape[1]
    parts = direct_parts(jnp.concatenate([first, second]), 1, section)
    place = ring_place(1)
    (block,) = unwritten(jax.ShapeDtypeStruct((SIDE * (count + rest), width), first.dtype))
    for steps, part in enumerate(parts):
        at = (place + steps) % SIDE
        block = lax.dynamic_update_slice(block, part[:count], (at * count, 0))
        block = lax.dynamic_update_slice(block, part[count:], (SIDE * count + at * rest, 0))
    half = SIDE * count
    own, after, before, upper, lower = ring_pieces(block, 0, section, half)
    wholes = (own, after, before)
    firsts = [part[:half] for part in wholes] + [upper]
    seconds = [part[half:] for part in wholes] + [lower]
    return (
        [part.reshape(SIDE, count, width) for part in firsts],
        [part.reshape(SIDE, rest, width) for part in seconds],
    )


def in_place_order(blocks):
    place = ring_place(0)
    (whole,) = unwritten(jax.ShapeDtypeStruct((SIDE,) + blocks[0].shape, blocks[0].dtype))
    for steps, block in zip((0, 1, 3, 2), blocks):
        whole = lax.dynamic_update_index_in_dim(whole, block, (place + steps) % SIDE, 0)
    return whole


def spread(piece):
    return lax.all_to_all(jnp.tile(piece, (SIDE * SIDE, 1)), "dp", 0, 0, tiled=True)


def summed_piece(pieces):
    taken = lax.all_to_all(pieces, "dp", 0, 0, tiled=True)
    return jnp.sum(taken.astype(F32), axis=0).astype(BF)


CUTS = (0, 576, 768, 1536, 1792, 1920)


def gathered(quarters, down, section):
    share = lax.dynamic_index_in_dim(quarters, ring_place(0), 0, keepdims=False)
    taken = to_chip(share, section)
    own_core = (to_core(quarters, section), to_core(down, section))
    own_core, taken, later = lax.optimization_barrier((own_core, taken, down))
    other_down = to_chip(later, section)
    own, after, before, upper, lower = ring_pieces(taken, 0, section)
    place = ring_place(0)
    other = jnp.zeros(quarters.shape, quarters.dtype)
    for steps, part in ((0, own), (1, after), (3, before)):
        other = lax.dynamic_update_index_in_dim(other, part, (place + steps) % SIDE, 0)
    other = lax.dynamic_update_slice(other, upper[None], ((place + 2) % SIDE, 0, 0))
    other = lax.dynamic_update_slice(other, lower[None], ((place + 2) % SIDE, upper.shape[0], 0))
    other_down, other = lax.optimization_barrier((other_down, other))
    return (*own_core, other, other_down, to_core(other, section), to_core(other_down, section))


def dot(left, right):
    return jnp.dot(left, right, preferred_element_type=F32)


def dot_t(left, right):
    return lax.dot_general(left, right, (((1,), (1,)), ((), ())), preferred_element_type=F32)


def t_dot(left, right):
    return lax.dot_general(left, right, (((0,), (0,)), ((), ())), preferred_element_type=F32)


def normalized(values):
    centered = values - jnp.mean(values, axis=-1, keepdims=True)
    spread = jnp.mean(centered * centered, axis=-1, keepdims=True)
    scale = lax.rsqrt(spread + EPSILON)
    return (centered * scale, scale)


def norm_backward(grad, values, gain):
    unit, scale = normalized(values)
    inner = grad * gain
    drop = jnp.mean(inner, axis=-1, keepdims=True)
    slope = jnp.mean(inner * unit, axis=-1, keepdims=True)
    return (
        scale * (inner - drop - unit * slope),
        jnp.sum(grad * unit, axis=0),
        jnp.sum(grad, axis=0),
    )


SLOPE = 0.7978845608028654
CUBIC = 0.044715


def one_hot(indices, names):
    return (indices[..., None] == names).astype(BF)


def by_tile(wide):
    return jnp.stack([wide[:, at : at + TILE] for at in range(0, wide.shape[1], TILE)])


def from_tiles(tiled):
    return jnp.concatenate(list(tiled), axis=1)


def heads_of(mixed):
    shaped = mixed.reshape(mixed.shape[0], -1, 3, 3, HEAD_DIM, TILE)
    return [shaped[:, :, part] for part in range(3)]


def attend(mixed, marks):
    q, k, v = heads_of(mixed)
    group, order = marks[:, 0].reshape(-1, TILE), marks[:, 1].reshape(-1, TILE)
    allowed = (group[:, :, None] == group[:, None, :]) & (order[:, None, :] <= order[:, :, None])
    scores = jnp.einsum("tsheq,tshek->tshqk", q, k, preferred_element_type=F32) * HEAD_DIM**-0.5
    scores = jnp.where(allowed[:, None, None], scores, -1e30)
    raised = jnp.exp(scores - jnp.max(scores, axis=-1, keepdims=True))
    shares = raised / jnp.sum(raised, axis=-1, keepdims=True)
    mixture = jnp.einsum("tshqk,tshek->tsheq", shares.astype(BF), v, preferred_element_type=F32)
    return (from_tiles(mixture.astype(BF).reshape(mixed.shape[0], -1, TILE)), shares)


def attend_back(mixed, shares, grad):
    q, k, v = heads_of(mixed)
    scale = HEAD_DIM**-0.5
    grad = by_tile(grad).reshape(q.shape)
    slopes = jnp.einsum("tsheq,tshek->tshqk", grad, v, preferred_element_type=F32)
    scores = (shares * (slopes - jnp.sum(shares * slopes, axis=-1, keepdims=True))).astype(BF)
    grads = [
        jnp.einsum("tshqk,tshek->tsheq", scores, k, preferred_element_type=F32) * scale,
        jnp.einsum("tshqk,tsheq->tshek", scores, q, preferred_element_type=F32) * scale,
        jnp.einsum("tshqk,tsheq->tshek", shares.astype(BF), grad, preferred_element_type=F32),
    ]
    return from_tiles(jnp.stack([part.astype(BF) for part in grads], axis=2).reshape(mixed.shape))


def gelu_pair(upper):
    upper = lax.optimization_barrier(upper)
    square = upper * upper
    bend = jnp.tanh(SLOPE * upper * (1.0 + CUBIC * square))
    near = 0.5 * (1.0 + bend)
    slope = near + 0.5 * SLOPE * upper * (1.0 - bend * bend) * (1.0 + 3 * CUBIC * square)
    return lax.optimization_barrier(((upper * near).astype(BF), slope))


def local_layer(rows, grad_result, weights, gains, marks):
    qkv_t, out, up_t, down, up_bias = weights
    unit, scale = normalized(rows)
    normed = (unit * gains[0] + gains[1]).astype(BF)
    mixed = by_tile(dot_t(qkv_t, normed).astype(BF))
    mixture, shares = attend(mixed, marks)
    middle = rows + t_dot(mixture, out)
    normed_mlp = (normalized(middle)[0] * gains[2] + gains[3]).astype(BF)
    active, slope = gelu_pair(dot_t(normed_mlp, up_t) + up_bias)
    result = (middle + dot(active, down) + gains[4]).astype(BF)
    grad_branch = grad_result.astype(BF)
    grad_upper = lax.optimization_barrier((slope * dot_t(grad_branch, down)).astype(BF))
    from_norm, *mlp_sums = norm_backward(dot(grad_upper, up_t), middle, gains[2])
    grad_middle = grad_result + from_norm
    grad_middle_low = grad_middle.astype(BF)
    grad_mixed = attend_back(mixed, shares, dot_t(out, grad_middle_low).astype(BF))
    from_norm, *attn_sums = norm_backward(t_dot(grad_mixed, qkv_t), rows, gains[0])
    grad_rows = (grad_middle + from_norm).astype(BF)
    sums = attn_sums + mlp_sums + [jnp.sum(grad_branch.astype(F32), axis=0)]
    vectors = jnp.concatenate([jnp.stack(sums), jnp.zeros((3, WIDTH), F32)])
    up_sums = jnp.sum(grad_upper.astype(F32), axis=0)
    stored = (normed, mixture, normed_mlp, active, grad_branch, grad_upper, grad_middle_low, grad_mixed)
    return (result, grad_rows, stored, vectors, up_sums)


def placed_bytes(mine, theirs, chip, core):
    rows, width = mine[0].shape[1] // 4, mine[0].shape[2]
    whole = jnp.zeros((8, SIDE, SIDE * rows, width), F32)
    for blocks, of_core, place in ((mine, core, ring_place(0)), (theirs, 1 - core, ring_place(1))):
        for steps, block in zip((0, 1, 3, 2), blocks):
            parts = block.reshape(SIDE, 2, 2, rows, width)
            for chips in range(2):
                part = jnp.swapaxes(parts[:, chips], 0, 1).reshape(2, 1, SIDE * rows, width)
                at = 4 * (chip ^ chips) + 2 * of_core
                whole = lax.dynamic_update_slice(
                    whole, part.astype(F32), (at, (place + steps) % SIDE, 0, 0)
                )
    return whole


def local(
    tokens,
    doc_lengths,
    byte_embed,
    patch_maps,
    attn_gain,
    attn_shift,
    qkv_weight,
    out_weight,
    mlp_gain,
    mlp_shift,
    up_weight,
    up_bias,
    down_weight,
    down_bias,
    cotangent,
):
    packs = tokens.shape[0]
    patches = tokens.shape[1] // PATCH
    own = patches // 4
    own_rows = packs * own
    rank = lax.axis_index("tensor")
    chip, core = rank // 2, rank % 2
    first_section = lax.axis_index("section") == 0
    embed, mapping = byte_embed[0], patch_maps[0]
    ranks = [rank ^ mask for mask in RELATIVE]
    gains = (attn_gain[0], attn_shift[0], mlp_gain[0], mlp_shift[0], down_bias[0])
    qkv_t = qkv_weight[0].reshape(WIDTH, 576).T
    up_t = up_weight[0].T
    out, down = out_weight[0], down_weight[0]

    places = jnp.arange(tokens.shape[1], dtype=jnp.int32)
    ends = jnp.cumsum(doc_lengths, axis=1)
    docs = jnp.sum((ends[:, None, :] <= places[None, :, None]).astype(jnp.int32), axis=2)
    names = jnp.arange(VOCAB, dtype=jnp.int32)

    def by_rank(values):
        quarters = values.reshape((packs, 4, own) + values.shape[2:])
        return jnp.stack(
            [lax.dynamic_index_in_dim(quarters, r, 1, keepdims=False) for r in ranks], axis=1
        )

    def to_own(partial):
        blocks = partial.astype(BF).reshape(packs, 4, own, WIDTH)
        pair = added(blocks[:, :2], to_core(blocks[:, 2:], 0))
        mine = pair[:, 0].astype(F32) + to_chip(pair[:, 1], 0).astype(F32)
        return mine.reshape(own_rows, WIDTH)

    def to_all(partial):
        blocks = partial.astype(BF).reshape(packs, 2, 2, own, WIDTH)
        pair = added(blocks, to_core(blocks, 0)[:, ::-1])
        whole = pair.astype(F32) + to_chip(pair, 0)[:, :, ::-1].astype(F32)
        return whole.reshape(-1, WIDTH)

    grouped = tokens.reshape(packs, patches, PATCH)
    before = jnp.concatenate([jnp.full((packs, 1, PATCH), -1, jnp.int32), grouped[:, :-1]], axis=1)
    before = by_rank(before).reshape(packs * patches, PATCH).T
    patch_rank = by_rank(jnp.broadcast_to(jnp.arange(patches, dtype=jnp.int32), (packs, patches)))
    global_marks = jnp.stack(
        [by_rank(docs[:, ::PATCH]).reshape(-1), patch_rank.reshape(-1)], axis=1
    )

    def mine_of(rows):
        return rows.reshape(packs, 4, own, -1)[:, 0].reshape(own_rows, -1)

    def global_pass():
        picked = one_hot(before, names)
        embedded = dot(picked.reshape(-1, VOCAB), embed).astype(BF).reshape(PATCH, -1, WIDTH)
        global_in = dot(jnp.concatenate(list(embedded), axis=1), mapping)
        normed = (normalized(global_in)[0] * gains[0] + gains[1]).astype(BF)
        mixed = by_tile(dot_t(qkv_t, normed).astype(BF))
        mixture, shares = attend(mixed, global_marks)
        middle = global_in + to_all(t_dot(mixture, out))
        normed_mlp = (normalized(middle)[0] * gains[2] + gains[3]).astype(BF)
        active, slope = gelu_pair(dot_t(normed_mlp, up_t) + up_bias)
        hidden = (mine_of(middle) + to_own(dot(active, down)) + gains[4]).astype(BF)
        return (hidden, (global_in, normed, mixed, mixture, middle, normed_mlp, slope, active, shares))

    def weights_of_all():
        bias_high = up_bias.astype(BF)
        bias_rest = up_bias - bias_high.astype(F32)
        bias_middle = bias_rest.astype(BF)
        bias_low = (bias_rest - bias_middle.astype(F32)).astype(BF)
        bias_rows = jnp.pad(jnp.concatenate([bias_high, bias_middle, bias_low]), ((0, 125), (0, 0)))
        some = CUTS[4] - CUTS[3]
        quarters = jnp.concatenate([qkv_t, out, up_t, down[:some], bias_rows]).reshape(4, -1, WIDTH)
        core_rows, *rest = gathered(quarters, down[some:], 1)
        core_rows = core_rows.reshape(-1, WIDTH)
        families = [core_rows[start:stop] for start, stop in zip(CUTS, CUTS[1:])]
        return (*families, *rest)

    def in_first():
        return global_pass() + (unwritten(*jax.eval_shape(weights_of_all)),)

    def in_second():
        first, rest = jax.eval_shape(global_pass)
        return (jnp.zeros(first.shape, first.dtype), tuple(unwritten(*rest)), list(weights_of_all()))

    hidden, global_stored, full = lax.cond(first_section, in_first, in_second)
    arrived = send(hidden, lambda y, z, s, t: (y, z, 1, t), (0,))
    global_out = jnp.where(first_section, hidden, arrived).reshape(packs, own, WIDTH)

    own_bytes = own * PATCH
    own_tokens = lax.dynamic_slice_in_dim(tokens, rank * own_bytes, own_bytes, 1)
    own_docs = lax.dynamic_slice_in_dim(docs, rank * own_bytes, own_bytes, 1)
    spot = jnp.arange(own_bytes, dtype=jnp.int32)
    earlier = jnp.where(spot % PATCH == 0, -1, jnp.roll(own_tokens, 1, axis=1)).reshape(-1, 1)
    group = (spot // PATCH) * 16 + own_docs
    rank_in = jnp.broadcast_to(spot % PATCH, group.shape)
    local_marks = jnp.stack([group.reshape(-1), rank_in.reshape(-1)], axis=1)
    *core_families, core_down, other_rows, other_down, other_core_rows, other_core_down = full

    def cut(rows):
        rows = rows.reshape(-1, WIDTH)
        return [rows[start:stop] for start, stop in zip(CUTS, CUTS[1:])]

    others = [cut(other_rows), core_families, cut(other_core_rows)]
    downs = (other_down, core_down, other_core_down)

    def family(own_part, at):
        return jnp.concatenate([own_part] + [parts[at] for parts in others])

    bias = jnp.concatenate(
        [up_bias] + [jnp.sum(parts[4][:3].astype(F32), axis=0, keepdims=True) for parts in others],
        axis=1,
    )
    weights = (
        family(qkv_t, 0),
        family(out, 1),
        family(up_t, 2),
        jnp.concatenate([down] + [part for pair in zip([p[3] for p in others], downs) for part in pair]),
        bias,
    )
    stream = dot_t(arrived, mapping).reshape(-1, WIDTH)
    local_in = stream + dot(one_hot(earlier[:, 0], names), embed)
    result_low, grad_rows, stored, vectors, up_sums = local_layer(
        local_in, cotangent.reshape(-1, WIDTH), weights, gains, local_marks
    )
    grad_hidden = dot(grad_rows.reshape(own_rows, PATCH * WIDTH), mapping).astype(BF)
    half_width = WIDTH // 2
    halves = result_low.reshape(packs, own_bytes, WIDTH)
    message = jnp.concatenate([halves[0, :, :half_width], halves[1, :, :half_width]], axis=1)
    message = jnp.concatenate([grad_hidden, message])
    given = send(message, lambda y, z, s, t: (y, z, 0, t), (1,))
    returned = [given[:own_rows]] + [
        send(grad_hidden, lambda y, z, s, t, mask=mask: (y, z, 0, t ^ mask), (1,))
        for mask in RELATIVE[1:]
    ]
    both_halves = jnp.stack([given[own_rows:, :half_width], given[own_rows:, half_width:]])
    local_out = jnp.where(first_section, both_halves, halves[..., half_width:])
    grad_bytes = jnp.swapaxes(grad_rows.reshape(own_rows, PATCH, WIDTH), 0, 1)
    normed, mixture, normed_mlp, active, grad_branch, grad_upper, grad_middle_low, grad_mixed = stored

    by_byte = grad_bytes.reshape(4, 2, own_rows, WIDTH)

    def bytes_of(mask):
        part = lax.dynamic_index_in_dim(by_byte, rank ^ mask, 0, keepdims=False)
        return jnp.concatenate([part, arrived[None]])

    shares = [
        send(bytes_of(mask), lambda y, z, s, t, mask=mask: (y, z, s, t ^ mask), (1,))
        if mask
        else bytes_of(mask)
        for mask in RELATIVE
    ]

    def shaped_out(grad_qkv, grad_out, grad_up, grad_down, small, grad_embed, grad_map):
        small = small.astype(F32)
        return (
            grad_embed[None],
            grad_map.reshape(1, -1, WIDTH),
            small[0][None],
            small[1][None],
            grad_qkv.T.astype(F32).reshape(1, WIDTH, 3, 192),
            grad_out.astype(F32)[None],
            small[2][None],
            small[3][None],
            grad_up.T.astype(F32)[None],
            small[5][None],
            grad_down.astype(F32)[None],
            small[4][None],
        )

    def global_tail():
        global_in, normed, mixed, mixture, middle, normed_mlp, slope, active, shares = global_stored
        grad_branch = jnp.stack(returned).reshape(4, packs, own, WIDTH).swapaxes(0, 1)
        grad_branch = grad_branch.reshape(-1, WIDTH)
        grad_upper = (slope * dot_t(grad_branch, down)).astype(BF)
        grad_up = t_dot(grad_upper, normed_mlp).astype(BF)
        grad_down = t_dot(active, grad_branch).astype(BF)
        from_norm, *mlp_sums = norm_backward(to_all(dot(grad_upper, up_t)), middle, gains[2])
        grad_middle = grad_branch.astype(F32) + from_norm
        grad_middle_low = grad_middle.astype(BF)
        grad_mixture = dot_t(out, grad_middle_low).astype(BF)
        grad_mixed = attend_back(mixed, shares, grad_mixture)
        from_norm, *attn_sums = norm_backward(to_all(t_dot(grad_mixed, qkv_t)), global_in, gains[0])
        grad_in = (grad_middle + from_norm).astype(BF)
        positions = lax.dynamic_slice_in_dim(before, rank * 2, 2, 0)
        counts = jnp.einsum(
            "jrv,rd->jvd", one_hot(positions, names), grad_in, preferred_element_type=F32
        ).astype(BF)
        small = jnp.stack(
            attn_sums
            + mlp_sums
            + [jnp.sum(grad_branch.astype(F32), axis=0), jnp.sum(grad_upper.astype(F32), axis=0)]
        )
        attn = jnp.concatenate(
            [dot(grad_mixed, normed).astype(BF), dot(mixture, grad_middle_low).astype(BF)]
        )
        pieces = jnp.concatenate(
            [
                grad_up.reshape(16, 48, WIDTH),
                grad_down.reshape(16, 48, WIDTH),
                attn.reshape(16, 48, WIDTH),
                jnp.pad(small, ((0, 122), (0, 0))).astype(BF).reshape(16, 8, WIDTH),
                jnp.swapaxes(counts.reshape(2, 16, 16, WIDTH), 0, 1).reshape(16, 32, WIDTH),
            ],
            axis=1,
        )
        piece = summed_piece(pieces)
        piece = jnp.concatenate([piece, to_chip(piece[152:], 0)])
        summed = spread(piece).reshape(16, 216, WIDTH)
        counts = jnp.swapaxes(summed[:, 152:].reshape(16, 4, 16, WIDTH), 0, 1).reshape(4, VOCAB, WIDTH)
        counts = in_order(counts, to_core(counts, 0))
        grad_up, grad_down, attn = [
            summed[:, start : start + 48].reshape(WIDTH, WIDTH) for start in (0, 48, 96)
        ]
        small = summed[0, 144:152]
        by_byte = mapping.reshape(PATCH, WIDTH, WIDTH)
        grad_map = jnp.einsum("vd,jve->jde", embed, counts, preferred_element_type=F32)
        grad_embed = jnp.einsum("jve,jde->vd", counts, by_byte, preferred_element_type=F32)
        return shaped_out(attn[:576], attn[576:], grad_up, grad_down, small, grad_embed, grad_map)

    def in_order(mine, theirs):
        shape = (2, 2) + mine.shape[1:]
        both = jnp.stack([mine.reshape(shape), theirs.reshape(shape)], axis=1)
        both = jnp.where(core == 0, both, both[:, ::-1])
        return jnp.where(chip == 0, both, both[::-1]).reshape((8,) + mine.shape[1:])

    def local_tail():
        products = (
            (grad_upper, normed_mlp),
            (active, grad_branch),
            (grad_mixed, normed),
            (mixture, grad_middle_low),
        )
        def product(left, right, half):
            if left.shape[1] == right.shape[0]:
                size = left.shape[0] // 2
                return dot(left[half * size : (half + 1) * size], right)
            size = left.shape[1] // 2
            return t_dot(left[:, half * size : (half + 1) * size], right)

        takens = [to_core(product(left, right, 1).astype(BF), 1) for left, right in products]
        embed_sums = t_dot(one_hot(earlier[:, 0], names), grad_rows).reshape(2, VOCAB // 2, WIDTH)
        ups = up_sums.reshape(2, 2, WIDTH)

        def half_with(half, up_sums):
            half = lax.dynamic_index_in_dim(embed_sums, half, 0, keepdims=False)
            return jnp.concatenate([half, vectors, up_sums, jnp.zeros((6, WIDTH), F32)])

        few_taken = to_core(half_with(1 - core, ups[1]).astype(BF), 1)

        both = jnp.pad(half_with(core, ups[0]) + few_taken.astype(F32), ((0, 112), (0, 0)))
        misc = jnp.stack([both, jnp.concatenate([both[:136], both[137:138], both[137:]])]).astype(BF)

        grad_up, grad_down, grad_qkv, grad_out = [
            added(product(left, right, 0), taken).reshape(2, -1, 48, WIDTH)
            for (left, right), taken in zip(products, takens)
        ]
        stacked = jnp.stack(shares)
        grad_map = jnp.einsum(
            "rkpd,rpe->kde", stacked[:, :2], stacked[:, 2], preferred_element_type=F32
        ).astype(BF)
        pieces = jnp.concatenate(
            [
                grad_up,
                grad_down,
                jnp.concatenate([grad_qkv, grad_out], axis=1),
                misc.reshape(2, 16, 16, WIDTH),
                grad_map.reshape(2, 16, 48, WIDTH),
            ],
            axis=2,
        )
        piece = plane_reduce(pieces, 1)
        taken = to_chip(jnp.concatenate([piece[1, :160], piece[0, 160:], piece[1, 160:]]), 1)
        piece = jnp.concatenate(
            [added(piece[0, :160], taken[:160]), piece[0, 160:], piece[1, 160:], taken[160:]]
        )
        maps, rows = plane_gather(piece[160:], piece[:160], 1)
        grad_map = placed_bytes(maps, [to_core(part, 1) for part in maps], chip, core)
        summed = in_place_order(rows).reshape(16, 160, WIDTH)
        grad_up, grad_down, attn = [
            summed[:, start : start + 48].reshape(WIDTH, WIDTH) for start in (0, 48, 96)
        ]
        misc = summed[:, 144:160].reshape(256, WIDTH)
        grad_embed, other = misc[:128], to_core(misc[:128], 1)
        grad_embed = jnp.concatenate(
            [jnp.where(core == 0, grad_embed, other), jnp.where(core == 0, other, grad_embed)]
        ).astype(F32)
        small = jnp.concatenate([misc[128:133], misc[136:137]])
        return shaped_out(attn[:576], attn[576:], grad_up, grad_down, small, grad_embed, grad_map)

    return (global_out, local_out) + lax.cond(first_section, global_tail, local_tail)


def solution(mesh):
    placed = (
        P("dp", None),
        P("dp", None),
        P("section", None, None),
        P("section", None, None),
        P("section", None),
        P("section", None),
        P("section", None, None, "tensor"),
        P("section", "tensor", None),
        P("section", None),
        P("section", None),
        P("section", None, "tensor"),
        P("section", "tensor"),
        P("section", "tensor", None),
        P("section", None),
        P("dp", "tensor", None),
    )
    return jax.shard_map(
        local,
        mesh=mesh,
        in_specs=placed,
        out_specs=(
            P("dp", "tensor", None),
            P("dp", "tensor", "section"),
            P("section", None, None),
            P("section", None, None),
            P("section", None),
            P("section", None),
            P("section", None, None, "tensor"),
            P("section", "tensor", None),
            P("section", None),
            P("section", None),
            P("section", None, "tensor"),
            P("section", "tensor"),
            P("section", "tensor", None),
            P("section", None),
        ),
        check_vma=False,
    )
```
